32 devices in a mesh: rows: 16 (over z, y, core), cols: 2 (over x).
Axes of the slice: x: 2, y: 2, z: 4, core: 2. Of those that a mesh axis runs over, the one named last changes fastest.
Arguments:
- images: float32 [128, 32, 128], P('rows'), may hold values from -6 to 6
- gauge_pixel: int32 [32768], P('rows'), may hold values from 0 to 32767
- row_mask: int32 [32768], P('rows'), may hold values 0 or 1
- gauge_counts: int32 [16], P('rows'), may hold values from 1 to 2048, as said below
- targets: float32 [32768], P('rows'), may hold values from -10 to 10
- theta: float32 [64, 8], replicated, may hold values from -2.5 to 2.5
- amplitude: float32 [64], replicated, may hold values from 0.5 to 1.5
- damping: float32 [], replicated, may hold values from 0.05 to 0.3
Outputs:
- r_factor: float32 [512, 512], replicated
- new_theta: float32 [64, 8], replicated
- predicted: float32 [32768], P(('rows', 'cols'))
The draws below stay inside these ranges and needn't reach their ends.
Inputs may be any that keep to these rules, and one draw needn't show every extreme that they name: The slots in use on an index of rows are its first gauge_counts slots; one index of rows uses all 2048.
All inputs are finite; a program needn't handle non-finite values. No bound on the sum of `row_mask` on one device may be relied on, other than what follows from the above.
Results may differ from the reference program's by a relative error of at most 0.0003.
Values sent between devices are 32-bit elements; how exact they have to be, the bound alone decides.
No kernel may reach another device: no remote copies, remote signals or barrier semaphores. Data moves between devices by JAX's collectives and lax.ppermute only.
A program may use at most 64 MiB of HBM per device.

```python
import math
import jax
import jax.numpy as jnp
from jax import lax

CH = 64
KB = 8
TH = 32
TW = 128
CLIP_DEV = 8
G_CAP = 2048
PARAMS = 512
ROW_GROUPS = 16
CLIPS = 128
GAUGES = 32768


def draw_gauge_counts(key, part):
    first_key = jax.random.fold_in(key, 11)
    second_key = jax.random.fold_in(key, 23)
    device_rank = jnp.arange(ROW_GROUPS)
    baseline = G_CAP // 3 + (G_CAP - G_CAP // 3) * device_rank // max(ROW_GROUPS - 1, 1)
    shortfall = jax.random.randint(first_key, (ROW_GROUPS,), 0, G_CAP // 8 + 1)
    fullest = jax.random.randint(second_key, (), 0, ROW_GROUPS)
    counts = jnp.where(device_rank == fullest, G_CAP, baseline - shortfall)
    return counts.astype(jnp.int32)


def place_ends(values, key, low, high):
    index_at = [jax.random.randint(jax.random.fold_in(key, axis), (), 0, length) for axis, length in enumerate(values.shape)]
    longest = values.shape.index(max(values.shape))
    next_to = index_at[:longest] + [(index_at[longest] + 1) % values.shape[longest]] + index_at[longest + 1:]
    return values.at[tuple(index_at)].set(low).at[tuple(next_to)].set(high)


def block_levels(stream_key, shape, shards, smallest, largest):
    def one(position, shards_of):
        draws = jax.random.uniform(jax.random.fold_in(jax.random.fold_in(stream_key, 6), position), (shards_of,), jnp.float32, smallest / len(shards), largest / len(shards))
        return jnp.repeat(jnp.exp(draws), shape[position] // shards_of).reshape((-1,) + (1,) * (len(shape) - position - 1))

    factor_of = one(*shards[0])
    for cut in shards[1:]:
        factor_of = factor_of * one(*cut)
    return factor_of


def bell_draw(stream_key, dims, scale, bound, cuts=(), kind=jnp.bfloat16):
    entries = jax.random.normal(stream_key, dims, jnp.float32) * scale
    if len(cuts) > 0:
        entries = block_levels(stream_key, dims, cuts, -0.22, 0.18) * entries
    return jnp.clip(entries, min=-bound, max=bound).astype(kind)


def setup_inputs(seed: int = 0) -> dict:
    seeds = jax.random.split(jax.random.key(seed), 9)
    return {
        "images": bell_draw(seeds[0], (CLIPS, TH, TW), 1.0, 6.0, ((0, 16),), jnp.float32),
        "gauge_pixel": place_ends(jax.random.randint(seeds[1], (GAUGES,), 0, CLIP_DEV * TH * TW), jax.random.fold_in(seeds[1], 1), 0, (CLIP_DEV * TH * TW) - 1).astype(jnp.int32),
        "row_mask": place_ends((jax.random.randint(seeds[2], (GAUGES,), 0, 8) < 7).astype(jnp.int32), jax.random.fold_in(seeds[2], 1), 0, 1),
        "gauge_counts": draw_gauge_counts(jax.random.fold_in(seeds[8], 71), 0),
        "targets": bell_draw(seeds[4], (GAUGES,), 2.0, 10.0, ((0, 16),), jnp.float32),
        "theta": bell_draw(seeds[5], (CH, KB), 0.35, 2.5, (), jnp.float32),
        "amplitude": jnp.clip(jnp.exp(jax.random.uniform(seeds[6], (CH,), jnp.float32, math.log(0.5), math.log(1.5))), 0.5, 1.5),
        "damping": jnp.clip(jnp.exp(jax.random.uniform(seeds[7], (), jnp.float32, math.log(0.05), math.log(0.3))), 0.05, 0.3),
    }


y_orders = [0, 1, 0, 2, 1, 0, 0, 0]
x_orders = [0, 0, 1, 0, 1, 2, 0, 2]
sigmas = [1.5, 1.5, 1.5, 1.5, 1.5, 1.5, 3.0, 3.0]

def kernel_values(spacing, deriv_order, width_sigma):
    envelope = jnp.exp(-spacing * spacing / (2.0 * width_sigma * width_sigma))
    if deriv_order == 1:
        return -spacing / width_sigma ** 2 * envelope
    if deriv_order == 2:
        return (spacing * spacing / width_sigma ** 4 - 1.0 / width_sigma ** 2) * envelope
    return envelope

def kernel_table(length, deriv_order, width_sigma):
    places = jnp.arange(length)
    spacing = (places[:, None] - places[None, :]).astype(jnp.float32)
    sample = jnp.arange(-12, 13).astype(jnp.float32)
    scaling = jnp.sqrt(jnp.sum(kernel_values(sample, deriv_order, width_sigma) ** 2))
    return kernel_values(spacing, deriv_order, width_sigma) / scaling

def features(clip_tiles):
    height = clip_tiles.shape[1]
    breadth = clip_tiles.shape[2]
    left_tabs = jnp.stack([kernel_table(height, y_orders[which], sigmas[which]) for which in range(8)])
    right_tabs = jnp.stack([kernel_table(breadth, x_orders[which], sigmas[which]) for which in range(8)])
    partial_conv = jnp.einsum('kij,cjw->kciw', left_tabs, clip_tiles, precision=lax.Precision.HIGHEST)
    full_conv = jnp.einsum('kciw,kvw->kciv', partial_conv, right_tabs, precision=lax.Precision.HIGHEST)
    return full_conv.reshape(full_conv.shape[0], -1)

def group_terms(clip_tiles, pixels, valid, count, measured, theta, amplitude):
    slots = pixels.shape[0]
    live = ((jnp.arange(slots) < count) & (valid == 1)).astype(jnp.float32)
    flat_feats = features(clip_tiles)
    phi = jnp.take(flat_feats, pixels, axis=1).T
    act = jnp.tanh(jnp.dot(phi, theta.T, precision=lax.Precision.HIGHEST))
    model = jnp.dot(act, amplitude, precision=lax.Precision.HIGHEST)
    resid = live * (model - measured)
    slope = live[:, None] * amplitude[None, :] * (1.0 - act * act)
    jac = (slope[:, :, None] * phi[:, None, :]).reshape(slots, -1)
    return (jac, resid, live)

def solve_step(lower, rhs):
    inner = lax.linalg.triangular_solve(lower, rhs[:, None], left_side=True, lower=True)
    outer = lax.linalg.triangular_solve(lower, inner, left_side=True, lower=True, transpose_a=True)
    return -outer[:, 0]

def reference(images, gauge_pixel, row_mask, gauge_counts, targets, theta, amplitude, damping):
    tiles = images.reshape(ROW_GROUPS, CLIP_DEV, TH, TW)
    pixels = gauge_pixel.reshape(ROW_GROUPS, G_CAP)
    valid = row_mask.reshape(ROW_GROUPS, G_CAP)
    measured = targets.reshape(ROW_GROUPS, G_CAP)
    inputs = (tiles, pixels, valid, gauge_counts, measured)

    def accumulate(carry, group):
        jac, resid, live = group_terms(group[0], group[1], group[2], group[3], group[4], theta, amplitude)
        gram = carry[0] + jnp.dot(jac.T, jac, precision=lax.Precision.HIGHEST)
        grad = carry[1] + jnp.dot(jac.T, resid, precision=lax.Precision.HIGHEST)
        return ((gram, grad, carry[2] + jnp.sum(live)), None)
    start = (jnp.zeros((PARAMS, PARAMS), jnp.float32), jnp.zeros((PARAMS,), jnp.float32), jnp.zeros((), jnp.float32))
    sums, unused = lax.scan(accumulate, start, inputs)
    gram, grad, total = sums
    normal = gram / total + damping * jnp.eye(PARAMS, dtype=jnp.float32)
    lower = jnp.linalg.cholesky(normal)
    step = solve_step(lower, grad / total)

    def predict(carry, group):
        jac, resid, live = group_terms(group[0], group[1], group[2], group[3], group[4], theta, amplitude)
        return (carry, resid + jnp.dot(jac, step, precision=lax.Precision.HIGHEST))
    unused_carry, predicted = lax.scan(predict, jnp.zeros((), jnp.float32), inputs)
    return (lower.T, theta + step.reshape(CH, KB), predicted.reshape(GAUGES))
```

```python
import functools
import math

import jax
import jax.numpy as jnp
from jax import lax
from jax.experimental import pallas as pl
from jax.experimental.pallas import tpu as pltpu
from jax.sharding import PartitionSpec as P

Y_ORDERS = [0, 1, 0, 2, 1, 0, 0, 0]
X_ORDERS = [0, 0, 1, 0, 1, 2, 0, 2]
SIGMAS = [1.5, 1.5, 1.5, 1.5, 1.5, 1.5, 3.0, 3.0]

F32 = jnp.float32
BF16 = jnp.bfloat16
NN = (((1,), (0,)), ((), ()))
NT = (((1,), (1,)), ((), ()))
VMEM = pl.BlockSpec(memory_space=pltpu.VMEM)
SMEM = pl.BlockSpec(memory_space=pltpu.SMEM)
PACK = 168
GROUP = 16
BLK = 64


def iota(shape, dim):
    return lax.broadcasted_iota(jnp.int32, shape, dim)


def kernel_scale(order, width):
    total = 0.0
    for t in range(-12, 13):
        e = math.exp(-t * t / (2.0 * width * width))
        if order == 1:
            e = -t / width**2 * e
        elif order == 2:
            e = (t * t / width**4 - 1.0 / width**2) * e
        total += e * e
    return 1.0 / math.sqrt(total)


def kernel_values(lag, order, width):
    e = jnp.exp(lag * lag * (-1.0 / (2.0 * width * width)))
    if order == 1:
        e = lag * (-1.0 / width**2) * e
    elif order == 2:
        e = (lag * lag * (1.0 / width**4) - 1.0 / width**2) * e
    return e * kernel_scale(order, width)


def split(a):
    hi = a.astype(BF16)
    return hi, (a - hi.astype(F32)).astype(BF16)


def dot(a, b, dims=NN):
    return lax.dot_general(a, b, dims, preferred_element_type=F32)


def dot3(a, b, dims=NN):
    ah, al = a if isinstance(a, tuple) else split(a)
    bh, bl = b if isinstance(b, tuple) else split(b)
    return dot(ah, bh, dims) + (dot(ah, bl, dims) + dot(al, bh, dims))


def dot_full(a, b, dims=NN):
    return lax.dot_general(
        a, b, dims, precision=lax.Precision.HIGHEST, preferred_element_type=F32
    )


def front(
    ncols,
    place_ref,
    count_ref,
    img_ref,
    pix_ref,
    mask_ref,
    target_ref,
    theta_ref,
    amp_ref,
    keep_ref,
    send_ref,
    slope_ref,
    phi_ref,
    resid_ref,
    feat_ref,
    jh_ref,
    jl_ref,
    all_phi_ref,
    all_sr_ref,
    all_slope_ref,
    all_resid_ref,
):
    half = place_ref[0]
    quarter = place_ref[1]
    column = place_ref[2]
    count = count_ref[0]
    slots = pix_ref.shape[1]
    rows, breadth = img_ref.shape
    height = 32
    chans, basis = theta_ref.shape

    image_t = split(img_ref[...].T)
    lefts = {}
    for order, width in sorted(set(zip(Y_ORDERS, SIGMAS))):
        lag = ((iota((height, breadth), 1) & (height - 1)) - iota((height, breadth), 0)).astype(F32)
        table = kernel_values(lag, order, width)
        wide = jnp.concatenate([table] * (rows // height), 0)
        wide = jnp.concatenate([wide] * (rows // breadth), 1)
        same = (iota((rows, rows), 0) // height) == (iota((rows, rows), 1) // height)
        lefts[order, width] = split(dot3(image_t, jnp.where(same, wide, 0.0)))
    lag = (iota((breadth, breadth), 0) - iota((breadth, breadth), 1)).astype(F32)
    for k in range(basis):
        right = kernel_values(lag, X_ORDERS[k], SIGMAS[k])
        hi, lo = split(dot3(right, lefts[Y_ORDERS[k], SIGMAS[k]]))
        feat_ref[k] = jnp.concatenate([hi, lo], 1)

    theta = theta_ref[...]
    diag = iota((chans, chans), 0) == iota((chans, chans), 1)
    amp = jnp.sum(jnp.where(diag, amp_ref[...], 0.0), axis=1, keepdims=True)

    chunk = min(512, slots)
    live_total = jnp.zeros((1, 1), F32)
    for start in range(0, slots, chunk):
        at = slice(start, start + chunk)
        pix = pix_ref[:, at]
        row = pix // breadth
        col = pix & (breadth - 1)
        pick_row = jnp.where(iota((rows, chunk), 0) == row, 1.0, 0.0).astype(BF16)
        pick_row = jnp.concatenate([pick_row, pick_row], 0)
        pick_col = iota((breadth, chunk), 0) == col
        phis = []
        for k in range(basis):
            found = dot(feat_ref[k], pick_row)
            phis.append(jnp.sum(jnp.where(pick_col, found, 0.0), axis=0, keepdims=True))
        phi = jnp.concatenate(phis, 0)
        all_phi_ref[:, at] = phi
        slot = iota((1, chunk), 1) + start
        live = jnp.where((slot < count) & (mask_ref[:, at] == 1), 1.0, 0.0)
        live_total = live_total + jnp.sum(live, axis=1, keepdims=True)
        z = theta[:, 0:1] * phis[0]
        for k in range(1, basis):
            z = z + theta[:, k : k + 1] * phis[k]
        act = jnp.tanh(z)
        model = jnp.sum(amp * act, axis=0, keepdims=True)
        resid = live * (model - target_ref[:, at])
        slope = (live * amp) * (1.0 - act * act)
        all_resid_ref[:, at] = resid
        all_slope_ref[:, at] = slope
        all_sr_ref[:, at] = slope * resid
        for k in range(basis):
            hi, lo = split(slope * phis[k])
            place = pl.multiple_of(((k + 4 * half) % basis) * chans, chans)
            jh_ref[pl.ds(place, chans), at] = hi
            jl_ref[pl.ds(place, chans), at] = lo

    own = slots // ncols
    mine = pl.ds(pl.multiple_of(column * own, own), own)
    slope_ref[...] = all_slope_ref[:, mine]
    phi_ref[...] = all_phi_ref[:, mine]
    resid_ref[...] = all_resid_ref[:, mine]

    grad = dot3(all_phi_ref[...], all_sr_ref[...], NT)

    packs = []
    for part in range(2):
        lo_row = 2 * part * chans
        a = slice(lo_row, lo_row + 2 * chans)
        b = slice(lo_row, lo_row + 6 * chans)
        blocks = dot3((jh_ref[a], jl_ref[a]), (jh_ref[b], jl_ref[b]), NT)
        first = blocks[:chans, : 5 * chans]
        second = blocks[chans:, chans:]
        r = iota((chans, 5 * chans), 0)
        c = iota((chans, 5 * chans), 1) & (chans - 1)
        fold = jnp.where(r >= c, first, second)
        lost = jnp.sum(jnp.where(r == c, second, 0.0), axis=0, keepdims=True)
        last = fold[:, 4 * chans :]
        extra = [lost[:, d * chans : (d + 1) * chans] for d in range(5)]
        extra.append(jnp.broadcast_to(live_total, (1, chans)))
        extra.append(jnp.zeros((2, chans), F32))
        tail = jnp.concatenate([grad, jnp.concatenate(extra, 0)], 1)
        packs.append(
            (
                fold[:, : 2 * chans],
                fold[:, 2 * chans : 4 * chans],
                jnp.concatenate([last[: chans // 2], last[chans // 2 :]], 1),
                tail,
            )
        )
    at = 0
    for one, two in zip(*packs):
        piece = pl.ds(at, one.shape[0])
        keep_ref[piece, :] = jnp.where(quarter == 0, one, two)
        send_ref[piece, :] = jnp.where(quarter == 0, two, one)
        at += one.shape[0]


def factor_block(work):
    tiles = [work[8 * t : 8 * t + 8] for t in range(BLK // 8)]
    sub = iota((8, 128), 0)

    def spread(x):
        return jnp.broadcast_to(x, (8, 128))

    for base in range(0, BLK, GROUP):
        t0 = base // 8
        left = range(t0, BLK // 8)
        cols = [
            {t: spread(tiles[t][:, base + m : base + m + 1]) for t in left} for m in range(GROUP)
        ]
        for m in range(GROUP):
            tp, s = (base + m) // 8, m % 8
            inverse = 1.0 / spread(cols[m][tp][s : s + 1])
            here = range(tp, BLK // 8)
            mult = {t: cols[m][t] * inverse for t in here}
            mult[tp] = jnp.where(sub > s, mult[tp], 0.0)
            for n in range(m + 1, GROUP):
                pivot_n = spread(cols[n][tp][s : s + 1])
                for t in here:
                    cols[n][t] = cols[n][t] - mult[t] * pivot_n
            pivot_row = spread(tiles[tp][s : s + 1])
            for t in here:
                tiles[t] = tiles[t] - mult[t] * pivot_row
    return jnp.concatenate(tiles, 0)


def back(
    place_ref,
    damping_ref,
    q0_ref,
    q1_ref,
    q2_ref,
    q3_ref,
    slope_ref,
    phi_ref,
    resid_ref,
    theta_ref,
    r_ref,
    new_theta_ref,
    pred_ref,
    pack_ref,
    plain_ref,
    mixed_ref,
    n_ref,
    inv_ref,
    x_ref,
):
    half = place_ref[0]
    quarter = place_ref[1]
    chans, basis = theta_ref.shape
    params = chans * basis
    pack_ref[2 * half + quarter] = q0_ref[...]
    pack_ref[2 * (1 - half) + quarter] = q1_ref[...]
    pack_ref[2 * half + (1 - quarter)] = q2_ref[...]
    pack_ref[2 * (1 - half) + (1 - quarter)] = q3_ref[...]

    total = pack_ref[0, PACK - 3 : PACK - 2, chans : chans + 1]
    scale = 1.0 / total
    r = iota((chans, chans), 0)
    c = iota((chans, chans), 1)

    def put(k, l, block):
        plain_ref[k * chans : (k + 1) * chans, l * chans : (l + 1) * chans] = block

    for q in range(4):
        tail = pack_ref[q, PACK - 8 :, chans:]
        folds = []
        for pair in range(2):
            f = pack_ref[q, pair * chans : (pair + 1) * chans, :]
            ft = f.T
            for d in range(2):
                folds.append((f[:, d * chans : (d + 1) * chans], ft[d * chans : (d + 1) * chans]))
        last = pack_ref[q, 2 * chans : 2 * chans + chans // 2, :]
        f = jnp.concatenate([last[:, :chans], last[:, chans:]], 0)
        folds.append((f, f.T))
        for d, (f, ft) in enumerate(folds):
            first = jnp.where(r >= c, f, ft)
            second = jnp.where(r < c, f, ft)
            second = jnp.where(r == c, tail[d : d + 1], second)
            k = 2 * q
            for k, block in ((2 * q, first), (2 * q + 1, second)):
                l = (k + d) % basis
                put(k, l, block)
                if d not in (0, 4):
                    put(l, k, block)
    tiles = params // 128
    per = 128 // chans
    for k in range(basis):
        for b in range(tiles):
            mixed_ref[b, pl.ds(k, chans, stride=basis), :] = plain_ref[
                k * chans : (k + 1) * chans, b * 128 : (b + 1) * 128
            ]
    for a in range(tiles):
        for b in range(tiles):
            t = mixed_ref[b, a * 128 : (a + 1) * 128, :].T * scale
            for e in range(per):
                n_ref[a, pl.ds(b * per + e, chans, stride=basis), :] = t[
                    e * chans : (e + 1) * chans
                ]
    grad = (pack_ref[0, PACK - 8 :, :] * scale).T[:chans]
    for k in range(basis):
        n_ref[tiles, pl.ds(k, chans, stride=basis), :] = jnp.broadcast_to(
            grad[:, k : k + 1], (chans, 128)
        )

    def load(at, first):
        return jnp.concatenate([n_ref[t, at, :] for t in range(first, tiles + 1)], 1)

    damping = damping_ref[0, 0]
    eye = iota((BLK, BLK), 0) == iota((BLK, BLK), 1)
    upper = iota((BLK, BLK), 0) <= iota((BLK, BLK), 1)
    blocks = params // BLK
    for j in range(blocks):
        at = slice(j * BLK, (j + 1) * BLK)
        first, skip = divmod(j * BLK, 128)
        a = n_ref[first, at, skip : skip + BLK] + jnp.where(eye, damping, 0.0)
        work = factor_block(jnp.concatenate([a, jnp.where(eye, 1.0, 0.0)], 1))
        pivots = jnp.sum(jnp.where(eye, work[:, :BLK], 0.0), axis=1, keepdims=True)
        work = work * lax.rsqrt(pivots)
        inverse = work[:, BLK:]
        inv_ref[j] = inverse
        panel = dot_full(inverse, load(at, first))
        x_ref[at, :] = panel[:, -128:]
        if first:
            r_ref[at, : first * 128] = jnp.zeros((BLK, first * 128), F32)
        r_ref[at, first * 128 :] = panel[:, :-128]
        r_ref[at, at] = jnp.where(upper, work[:, :BLK], 0.0)
        if skip:
            r_ref[at, first * 128 : j * BLK] = jnp.zeros((BLK, skip), F32)
        if j + 1 < blocks:
            nxt = (j + 1) * BLK // 128
            rest = panel[:, (nxt - first) * 128 :]
            update = dot_full(rest[:, :-128].T, rest)
            for t in range(nxt, tiles + 1):
                n_ref[t, nxt * 128 :, :] = (
                    n_ref[t, nxt * 128 :, :] - update[:, (t - nxt) * 128 : (t - nxt + 1) * 128]
                )

    for j in reversed(range(blocks)):
        at = slice(j * BLK, (j + 1) * BLK)
        y = x_ref[at, :]
        if j + 1 < blocks:
            y = y - dot_full(r_ref[at, (j + 1) * BLK :], x_ref[(j + 1) * BLK :, :])
        x_ref[at, :] = dot_full(inv_ref[j].T, y)

    lane = iota((chans, 128), 1)
    weight = jnp.zeros(slope_ref.shape, F32)
    move = jnp.zeros((chans, 128), F32)
    width = slope_ref.shape[1]
    for k in range(basis):
        step = -x_ref[pl.ds(k, chans, stride=basis), :]
        move = jnp.where(lane == k, step, move)
        wide = jnp.concatenate([step] * (width // 128), 1)
        weight = weight + wide * phi_ref[k : k + 1, :]
    new_theta_ref[...] = theta_ref[...] + move[:, :basis]
    pred_ref[...] = resid_ref[...] + jnp.sum(slope_ref[...] * weight, axis=0, keepdims=True)


def flips(size, bit):
    return [(i, i ^ bit) for i in range(size)]


def on_device(images, gauge_pixel, row_mask, gauge_counts, targets, theta, amplitude, damping):
    nrows = lax.axis_size("rows")
    ncols = lax.axis_size("cols")
    row = lax.axis_index("rows")
    column = lax.axis_index("cols")
    slots = gauge_pixel.shape[0]
    share = slots // ncols
    chans, basis = theta.shape
    params = chans * basis
    if ncols == 2:
        half, quarter = column, row % 2
    else:
        half, quarter = column // 2 % 2, column % 2
    place = jnp.stack([half, quarter, column]).astype(jnp.int32)
    shape = jax.ShapeDtypeStruct
    keep, send, slope, phi, resid = pl.pallas_call(
        functools.partial(front, ncols),
        out_shape=[
            shape((PACK, 128), F32),
            shape((PACK, 128), F32),
            shape((chans, share), F32),
            shape((basis, share), F32),
            shape((1, share), F32),
        ],
        in_specs=[SMEM, SMEM] + [VMEM] * 6,
        out_specs=[VMEM] * 5,
        scratch_shapes=[
            pltpu.VMEM((basis, 128, 512), BF16),
            pltpu.VMEM((params, slots), BF16),
            pltpu.VMEM((params, slots), BF16),
            pltpu.VMEM((basis, slots), F32),
            pltpu.VMEM((chans, slots), F32),
            pltpu.VMEM((chans, slots), F32),
            pltpu.VMEM((1, slots), F32),
        ],
        compiler_params=pltpu.CompilerParams(vmem_limit_bytes=40 * 2**20),
        name="front",
    )(
        place,
        gauge_counts,
        images.reshape(-1, images.shape[2]),
        gauge_pixel.reshape(1, slots),
        row_mask.reshape(1, slots),
        targets.reshape(1, slots),
        theta,
        amplitude.reshape(1, chans),
    )

    bit = 1
    if ncols == 2:
        keep = keep + lax.ppermute(send, "rows", flips(nrows, 1))
        bit = 2
    while bit < nrows:
        keep = keep + lax.ppermute(keep, "rows", flips(nrows, bit))
        bit *= 2
    if ncols == 2:
        other_half = lax.ppermute(keep, "cols", flips(ncols, 1))
        other_quarter = lax.ppermute(keep, "rows", flips(nrows, 1))
        other_both = lax.ppermute(other_half, "rows", flips(nrows, 1))
    else:
        other_half = lax.ppermute(keep, "cols", flips(ncols, 2))
        other_quarter = lax.ppermute(keep, "cols", flips(ncols, 1))
        other_both = lax.ppermute(other_half, "cols", flips(ncols, 1))

    r_factor, new_theta, predicted = pl.pallas_call(
        back,
        out_shape=[
            shape((params, params), F32),
            shape((chans, basis), F32),
            shape((1, share), F32),
        ],
        in_specs=[SMEM, SMEM] + [VMEM] * 8,
        out_specs=[VMEM] * 3,
        scratch_shapes=[
            pltpu.VMEM((4, PACK, 128), F32),
            pltpu.VMEM((params, params), F32),
            pltpu.VMEM((params // 128, params, 128), F32),
            pltpu.VMEM((params // 128 + 1, params, 128), F32),
            pltpu.VMEM((params // BLK, BLK, BLK), F32),
            pltpu.VMEM((params, 128), F32),
        ],
        compiler_params=pltpu.CompilerParams(vmem_limit_bytes=40 * 2**20),
        name="back",
    )(
        place,
        damping.reshape(1, 1),
        keep,
        other_half,
        other_quarter,
        other_both,
        slope,
        phi,
        resid,
        theta,
    )
    return r_factor, new_theta, predicted.reshape(share)


def solution(mesh):
    return jax.shard_map(
        on_device,
        mesh=mesh,
        in_specs=(P("rows", None, None), P("rows"), P("rows"), P("rows"), P("rows"), P(), P(), P()),
        out_specs=(P(), P(), P(("rows", "cols"))),
        check_vma=False,
    )
```

```python
import functools
import math

import jax
import jax.numpy as jnp
from jax import lax
from jax.experimental import pallas as pl
from jax.experimental.pallas import tpu as pltpu
from jax.sharding import PartitionSpec as P

Y_ORDERS = [0, 1, 0, 2, 1, 0, 0, 0]
X_ORDERS = [0, 0, 1, 0, 1, 2, 0, 2]
SIGMAS = [1.5, 1.5, 1.5, 1.5, 1.5, 1.5, 3.0, 3.0]

F32 = jnp.float32
BF16 = jnp.bfloat16
NN = (((1,), (0,)), ((), ()))
NT = (((1,), (1,)), ((), ()))
VMEM = pl.BlockSpec(memory_space=pltpu.VMEM)
HBM = pl.BlockSpec(memory_space=pltpu.HBM)
SMEM = pl.BlockSpec(memory_space=pltpu.SMEM)
PACK = 176
CHUNK = 512
AHEAD = 2
BLK = 64


def iota(shape, dim):
    return lax.broadcasted_iota(jnp.int32, shape, dim)


def kernel_scale(order, width):
    total = 0.0
    for t in range(-12, 13):
        e = math.exp(-t * t / (2.0 * width * width))
        if order == 1:
            e = -t / width**2 * e
        elif order == 2:
            e = (t * t / width**4 - 1.0 / width**2) * e
        total += e * e
    return 1.0 / math.sqrt(total)


def kernel_values(lag, order, width):
    e = jnp.exp(lag * lag * (-1.0 / (2.0 * width * width)))
    if order == 1:
        e = lag * (-1.0 / width**2) * e
    elif order == 2:
        e = (lag * lag * (1.0 / width**4) - 1.0 / width**2) * e
    return e * kernel_scale(order, width)


def split(a):
    hi = a.astype(BF16)
    return hi, (a - hi.astype(F32)).astype(BF16)


def dot(a, b, dims=NN):
    return lax.dot_general(a, b, dims, preferred_element_type=F32)


def dot3(a, b, dims=NN):
    ah, al = a if isinstance(a, tuple) else split(a)
    bh, bl = b if isinstance(b, tuple) else split(b)
    return dot(ah, bh, dims) + (dot(ah, bl, dims) + dot(al, bh, dims))


def dot_full(a, b, dims=NN):
    return lax.dot_general(
        a, b, dims, precision=lax.Precision.HIGHEST, preferred_element_type=F32
    )


mm = dot_full


def places(ncols):
    column = lax.axis_index("cols")
    if ncols == 2:
        return column, lax.axis_index("rows") & 1, column
    return (column >> 1) & 1, column & 1, column


def front(
    ncols,
    count_ref,
    img_hbm,
    pix_hbm,
    mask_hbm,
    target_hbm,
    theta_hbm,
    amp_hbm,
    keep_ref,
    send_ref,
    slope_ref,
    phi_ref,
    resid_ref,
    img_ref,
    pix_ref,
    mask_ref,
    target_ref,
    theta_ref,
    amp_ref,
    pick_ref,
    feat_ref,
    jac_ref,
    all_phi_ref,
    all_sr_ref,
    all_slope_ref,
    all_resid_ref,
    sem,
):
    pairs = [
        (img_hbm, img_ref),
        (pix_hbm, pix_ref),
        (theta_hbm, theta_ref),
        (amp_hbm, amp_ref),
        (mask_hbm, mask_ref),
        (target_hbm, target_ref),
    ]
    copies = [pltpu.make_async_copy(a, b, sem.at[i]) for i, (a, b) in enumerate(pairs)]
    for copy in copies:
        copy.start()
    half, quarter, column = places(ncols)
    count = count_ref[0]
    slots = pix_ref.shape[1]
    rows, breadth = img_ref.shape
    height = 32
    basis, chans = theta_ref.shape
    params = basis * chans

    kinds = sorted(set(zip(Y_ORDERS, SIGMAS)))
    tables = []
    for order, width in kinds:
        lag = ((iota((height, breadth), 1) & (height - 1)) - iota((height, breadth), 0)).astype(F32)
        table = kernel_values(lag, order, width)
        wide = jnp.concatenate([table] * (rows // height), 0)
        wide = jnp.concatenate([wide] * (rows // breadth), 1)
        same = (iota((rows, rows), 0) // height) == (iota((rows, rows), 1) // height)
        tables.append(split(jnp.where(same, wide, 0.0)))
    lag = (iota((breadth, breadth), 0) - iota((breadth, breadth), 1)).astype(F32)
    rights = [split(kernel_values(lag, X_ORDERS[k], SIGMAS[k])) for k in range(basis)]
    copies[1].wait()
    chunk = min(CHUNK, slots)
    for start in range(0, slots, chunk):
        row = pix_ref[:, start : start + chunk] // breadth
        pick = jnp.where(iota((rows, chunk), 0) == row, 1.0, 0.0).astype(BF16)
        pick_ref[:rows, start : start + chunk] = pick
        pick_ref[rows:, start : start + chunk] = pick
    copies[0].wait()
    image_t = split(img_ref[...].T)
    lefts = {kind: split(dot3(image_t, table)) for kind, table in zip(kinds, tables)}
    for k in range(basis):
        hi, lo = split(dot3(rights[k], lefts[Y_ORDERS[k], SIGMAS[k]]))
        feat_ref[k * breadth : (k + 1) * breadth, :rows] = hi
        feat_ref[k * breadth : (k + 1) * breadth, rows:] = lo

    for copy in copies[2:]:
        copy.wait()
    theta = theta_ref[...].T
    diag = iota((chans, chans), 0) == iota((chans, chans), 1)
    amp = jnp.sum(jnp.where(diag, amp_ref[...], 0.0), axis=1, keepdims=True)

    live_total = jnp.zeros((1, 1), F32)
    for start in range(0, slots, chunk):
        at = slice(start, start + chunk)
        pick_col = iota((breadth, chunk), 0) == pix_ref[:, at] & (breadth - 1)
        phis = []
        for k in range(basis):
            found = dot(feat_ref[k * breadth : (k + 1) * breadth], pick_ref[:, at])
            phis.append(jnp.sum(jnp.where(pick_col, found, 0.0), axis=0, keepdims=True))
        phi = jnp.concatenate(phis, 0)
        all_phi_ref[:, at] = phi
        slot = iota((1, chunk), 1) + start
        live = jnp.where((slot < count) & (mask_ref[:, at] == 1), 1.0, 0.0)
        live_total = live_total + jnp.sum(live, axis=1, keepdims=True)
        z = theta[:, 0:1] * phis[0]
        for k in range(1, basis):
            z = z + theta[:, k : k + 1] * phis[k]
        act = jnp.tanh(z)
        model = jnp.sum(amp * act, axis=0, keepdims=True)
        resid = live * (model - target_ref[:, at])
        slope = (live * amp) * (1.0 - act * act)
        all_resid_ref[:, at] = resid
        all_slope_ref[:, at] = slope
        all_sr_ref[:, at] = slope * resid
        for k in range(basis):
            hi, lo = split(slope * phis[k])
            place = ((k + (basis // 2) * half) % basis) * chans
            jac_ref[pl.ds(pl.multiple_of(place, chans), chans), at] = hi
            jac_ref[pl.ds(pl.multiple_of(params + place, chans), chans), at] = lo

    own = slots // ncols
    mine = pl.ds(pl.multiple_of(column * own, own), own)
    slope_ref[...] = all_slope_ref[:, mine]
    phi_ref[...] = all_phi_ref[:, mine]
    resid_ref[...] = all_resid_ref[:, mine]

    grad = dot3(all_phi_ref[...], all_sr_ref[...], NT)

    four = basis // 2 * chans
    both = dot(jac_ref[:four], jac_ref[...], NT)
    low = dot(jac_ref[params : params + four], jac_ref[:params], NT)
    gram = both[:, :params] + (both[:, params:] + low)
    r = iota((chans, 128), 0)
    c = iota((chans, 128), 1) & (chans - 1)
    packs = []
    for part in range(2):
        tiles = [
            [
                gram[
                    (2 * part + e) * chans : (2 * part + e + 1) * chans,
                    (part + i) * 128 : (part + i + 1) * 128,
                ]
                for i in range(3)
            ]
            for e in range(2)
        ]
        spare = jnp.where(iota((chans, 128), 1) < chans, tiles[0][2], tiles[1][0])
        folds = []
        lost = []
        for one, two in (
            (tiles[0][0], tiles[0][1]),
            (tiles[1][1], tiles[1][2]),
            (spare, pltpu.roll(spare, chans, 1)),
        ):
            folds.append(jnp.where(r >= c, one, two))
            lost.append(jnp.sum(jnp.where(r == c, two, 0.0), axis=0, keepdims=True))
        last = folds.pop()
        folds.append(jnp.concatenate([last[: chans // 2, :chans], last[chans // 2 :, :chans]], 1))
        wide = jnp.broadcast_to(live_total, (1, 128))
        folds.append(jnp.concatenate(lost + [wide, jnp.zeros((4, 128), F32)], 0))
        folds.append(jnp.concatenate([grad, jnp.zeros((basis, 128 - chans), F32)], 1))
        packs.append(folds)
    at = 0
    for one, two in zip(*packs):
        piece = pl.ds(at, one.shape[0])
        keep_ref[piece, :] = jnp.where(quarter == 0, one, two)
        send_ref[piece, :] = jnp.where(quarter == 0, two, one)
        at += one.shape[0]


def factor_block(tiles, base):
    count = len(tiles)
    tiles = list(tiles)
    sub = iota((8, 128), 0)
    inverses = []

    def spread(x):
        return jnp.broadcast_to(x, (8, 128))

    def column(t, at):
        return spread(tiles[t][:, at : at + 1])

    ahead = {}
    for g in range(count):
        here = range(g, count)
        cols = {
            t: ahead[t] if t in ahead else [column(t, base + 8 * g + m) for m in range(8)]
            for t in here
        }
        ahead = {
            t: [column(t, base + 8 * g + 8 + m) for m in range(8)]
            for t in range(g + 1, min(g + 1 + AHEAD, count))
        }
        kept = jnp.zeros((8, 128), F32)
        for m in range(8):
            inverse = 1.0 / spread(cols[g][m][m : m + 1])
            kept = jnp.where(sub == m, inverse, kept)
            mult = {t: cols[t][m] * inverse for t in here}
            mult[g] = jnp.where(sub > m, mult[g], 0.0)
            for n in range(m + 1, 8):
                pivot = spread(cols[g][n][m : m + 1])
                for t in here:
                    cols[t][n] = cols[t][n] - mult[t] * pivot
            for n in range(8 if ahead else 0):
                pivot = spread(cols[g + 1][m][n : n + 1])
                for t in ahead:
                    ahead[t][n] = ahead[t][n] - mult[t] * pivot
            pivot = spread(tiles[g][m : m + 1])
            for t in here:
                tiles[t] = tiles[t] - mult[t] * pivot
        inverses.append(kept)
    return tiles, inverses


def back(
    ncols,
    damping_ref,
    q0_ref,
    q1_ref,
    q2_ref,
    q3_ref,
    slope_ref,
    phi_ref,
    resid_ref,
    theta_ref,
    r_ref,
    new_theta_ref,
    pred_ref,
    pack_ref,
    plain_ref,
    mixed_ref,
    n_ref,
    t_ref,
    x_ref,
):
    half, quarter, _ = places(ncols)
    basis, chans = theta_ref.shape
    params = chans * basis
    pack_ref[2 * half + quarter] = q0_ref[...]
    pack_ref[2 * (1 - half) + quarter] = q1_ref[...]
    pack_ref[2 * half + (1 - quarter)] = q2_ref[...]
    pack_ref[2 * (1 - half) + (1 - quarter)] = q3_ref[...]

    total = pack_ref[0, PACK - 13 : PACK - 12, :1]
    scale = 1.0 / total
    r = iota((chans, chans), 0)
    c = iota((chans, chans), 1)

    def put(k, l, block):
        plain_ref[k * chans : (k + 1) * chans, l * chans : (l + 1) * chans] = block

    for q in range(4):
        lost = pack_ref[q, PACK - 16 : PACK - 13, :]
        for i in range(2):
            fold = pack_ref[q, i * chans : (i + 1) * chans, :]
            turned = fold.T
            k = 2 * q + i
            for e in range(2):
                lane = slice(e * chans, (e + 1) * chans)
                f, ft = fold[:, lane], turned[lane]
                second = jnp.where(r == c, lost[i : i + 1, lane], jnp.where(r < c, f, ft))
                for d, block in ((i + e, jnp.where(r >= c, f, ft)), (i + e + 2, second)):
                    l = (k + d) % basis
                    put(k, l, block)
                    if d not in (0, basis // 2):
                        put(l, k, block)
        last = pack_ref[q, 2 * chans : 2 * chans + chans // 2, :]
        f = jnp.concatenate([last[:, :chans], last[:, chans:]], 0)
        ft = f.T
        put(2 * q, (2 * q + basis // 2) % basis, jnp.where(r >= c, f, ft))
        second = jnp.where(r == c, lost[2:, :chans], jnp.where(r < c, f, ft))
        put(2 * q + 1, 2 * q + 1, second)
    tiles = params // 128
    per = 128 // chans
    for k in range(basis):
        for b in range(tiles):
            mixed_ref[b, pl.ds(k, chans, stride=basis), :] = plain_ref[
                k * chans : (k + 1) * chans, b * 128 : (b + 1) * 128
            ]
    for a in range(tiles):
        for b in range(tiles):
            t = mixed_ref[b, a * 128 : (a + 1) * 128, :].T * scale
            for e in range(per):
                n_ref[a, pl.ds(b * per + e, chans, stride=basis), :] = t[
                    e * chans : (e + 1) * chans
                ]
    grad = (pack_ref[0, PACK - 8 :, :] * scale).T[:chans]
    for k in range(basis):
        n_ref[tiles, pl.ds(k, chans, stride=basis), :] = jnp.broadcast_to(
            grad[:, k : k + 1], (chans, 128)
        )

    damping = damping_ref[0, 0]
    for t in range(tiles):
        at = slice(t * 128, (t + 1) * 128)
        spot = iota((128, 128), 0) == iota((128, 128), 1)
        n_ref[t, at, :] = n_ref[t, at, :] + jnp.where(spot, damping, 0.0)

    lane = iota((BLK, 128), 1)
    sub = iota((BLK, 128), 0)
    zeros = jnp.zeros((BLK, 128), F32)

    def load(at, first):
        return jnp.concatenate([n_ref[t, at, :] for t in range(first, tiles + 1)], 1)

    def factor(block, base):
        eye = jnp.where(lane - (BLK - base) == sub, 1.0, 0.0)
        whole = jnp.where((lane >= base) & (lane < base + BLK), block, eye)
        parts, inverses = factor_block([whole[8 * t : 8 * t + 8] for t in range(BLK // 8)], base)
        return jnp.concatenate([p * (i * lax.rsqrt(i)) for p, i in zip(parts, inverses)], 0)

    for j in range(tiles):
        top = slice(j * 128, j * 128 + BLK)
        low = slice(j * 128 + BLK, (j + 1) * 128)
        if j:
            r_ref[j * 128 : (j + 1) * 128, : j * 128] = jnp.zeros((128, j * 128), F32)
        w0 = factor(n_ref[j, top, :], 0)
        inv0 = jnp.where(lane >= BLK, w0, 0.0)
        first = mm(inv0, jnp.concatenate([zeros, n_ref[j, top, :]], 0))
        r_ref[top, j * 128 : (j + 1) * 128] = jnp.where(
            lane >= BLK, first, jnp.where(lane >= sub, w0, 0.0)
        )
        cross = first[:, BLK:].T
        w1 = factor(n_ref[j, low, :] - mm(cross, first), BLK)
        r_ref[low, j * 128 : (j + 1) * 128] = jnp.where(lane - BLK >= sub, w1, 0.0)
        inv1 = w1[:, :BLK]
        over0 = load(top, j + 1)
        rest0 = mm(inv0, jnp.concatenate([jnp.zeros(over0.shape, F32), over0], 0))
        rest1 = mm(inv1, load(low, j + 1) - mm(cross, rest0))
        rest = jnp.concatenate([rest0, rest1], 0)
        if j + 1 < tiles:
            r_ref[j * 128 : (j + 1) * 128, (j + 1) * 128 :] = rest[:, :-128]
            for i in range(j + 1, tiles):
                begin = (i - j - 1) * 128
                turned = rest[:, begin : begin + 128].T
                update = mm(turned, rest[:, begin:])
                at = slice(i * 128, (i + 1) * 128)
                for t in range(i, tiles + 1):
                    n_ref[t, at, :] = n_ref[t, at, :] - update[:, (t - i) * 128 : (t - i + 1) * 128]
        turn1 = mm(w1.T[:BLK], rest1)
        whole0 = mm(w0.T[BLK:], jnp.concatenate([first, rest0], 1))
        link = jnp.where(lane >= BLK, whole0[:, :128], 0.0)
        turn0 = whole0[:, 128:] - mm(
            link, jnp.concatenate([jnp.zeros(turn1.shape, F32), turn1], 0)
        )
        turn = jnp.concatenate([turn0, turn1], 0)
        for t in range(j + 1, tiles + 1):
            t_ref[j, t] = turn[:, (t - j - 1) * 128 : (t - j) * 128]

    for j in reversed(range(tiles)):
        x = t_ref[j, tiles]
        if j + 1 < tiles:
            x = x - mm(
                jnp.concatenate([t_ref[j, t] for t in range(j + 1, tiles)], 1),
                x_ref[(j + 1) * 128 :, :],
            )
        x_ref[j * 128 : (j + 1) * 128, :] = x

    lane = iota((chans, 128), 1)
    weight = jnp.zeros(slope_ref.shape, F32)
    move = jnp.zeros((chans, 128), F32)
    width = slope_ref.shape[1]
    for k in range(basis):
        step = -x_ref[pl.ds(k, chans, stride=basis), :]
        move = jnp.where(lane == k, step, move)
        wide = jnp.concatenate([step] * (width // 128), 1)
        weight = weight + wide * phi_ref[k : k + 1, :]
    new_theta_ref[...] = theta_ref[...] + move.T[:basis]
    pred_ref[...] = resid_ref[...] + jnp.sum(slope_ref[...] * weight, axis=0, keepdims=True)


def flips(size, bit):
    return [(i, i ^ bit) for i in range(size)]


def on_device(images, gauge_pixel, row_mask, gauge_counts, targets, theta, amplitude, damping):
    nrows = lax.axis_size("rows")
    ncols = lax.axis_size("cols")
    slots = gauge_pixel.shape[0]
    share = slots // ncols
    chans, basis = theta.shape
    params = chans * basis
    breadth = images.shape[2]
    pixel_rows = images.shape[0] * images.shape[1]
    theta_t = theta.T
    shape = jax.ShapeDtypeStruct
    keep, send, slope, phi, resid = pl.pallas_call(
        functools.partial(front, ncols),
        out_shape=[
            pltpu.VMEM((PACK, 128), F32),
            pltpu.VMEM((PACK, 128), F32),
            pltpu.VMEM((chans, share), F32),
            pltpu.VMEM((basis, share), F32),
            pltpu.VMEM((1, share), F32),
        ],
        in_specs=[SMEM] + [HBM] * 6,
        out_specs=[VMEM] * 5,
        scratch_shapes=[
            pltpu.VMEM((pixel_rows, breadth), F32),
            pltpu.VMEM((1, slots), jnp.int32),
            pltpu.VMEM((1, slots), jnp.int32),
            pltpu.VMEM((1, slots), F32),
            pltpu.VMEM((basis, chans), F32),
            pltpu.VMEM((1, chans), F32),
            pltpu.VMEM((2 * pixel_rows, slots), BF16),
            pltpu.VMEM((basis * breadth, 2 * pixel_rows), BF16),
            pltpu.VMEM((2 * params, slots), BF16),
            pltpu.VMEM((basis, slots), F32),
            pltpu.VMEM((chans, slots), F32),
            pltpu.VMEM((chans, slots), F32),
            pltpu.VMEM((1, slots), F32),
            pltpu.SemaphoreType.DMA((6,)),
        ],
        compiler_params=pltpu.CompilerParams(vmem_limit_bytes=60 * 2**20),
        name="front",
    )(
        gauge_counts,
        images.reshape(pixel_rows, breadth),
        gauge_pixel.reshape(1, slots),
        row_mask.reshape(1, slots),
        targets.reshape(1, slots),
        theta_t,
        amplitude.reshape(1, chans),
    )

    bit = 1
    if ncols == 2:
        keep = keep + lax.ppermute(send, "rows", flips(nrows, 1))
        bit = 2
    while bit < nrows:
        keep = keep + lax.ppermute(keep, "rows", flips(nrows, bit))
        bit *= 2
    if ncols == 2:
        other_half = lax.ppermute(keep, "cols", flips(ncols, 1))
        other_quarter = lax.ppermute(keep, "rows", flips(nrows, 1))
        other_both = lax.ppermute(other_half, "rows", flips(nrows, 1))
    else:
        other_half = lax.ppermute(keep, "cols", flips(ncols, 2))
        other_quarter = lax.ppermute(keep, "cols", flips(ncols, 1))
        other_both = lax.ppermute(other_half, "cols", flips(ncols, 1))

    r_factor, new_theta, predicted = pl.pallas_call(
        functools.partial(back, ncols),
        out_shape=[
            shape((params, params), F32),
            shape((basis, chans), F32),
            shape((1, share), F32),
        ],
        in_specs=[SMEM] + [VMEM] * 8,
        out_specs=[VMEM] * 3,
        scratch_shapes=[
            pltpu.VMEM((4, PACK, 128), F32),
            pltpu.VMEM((params, params), F32),
            pltpu.VMEM((params // 128, params, 128), F32),
            pltpu.VMEM((params // 128 + 1, params, 128), F32),
            pltpu.VMEM((params // 128, params // 128 + 1, 128, 128), F32),
            pltpu.VMEM((params, 128), F32),
        ],
        compiler_params=pltpu.CompilerParams(vmem_limit_bytes=40 * 2**20),
        name="back",
    )(
        damping.reshape(1, 1),
        keep,
        other_half,
        other_quarter,
        other_both,
        slope,
        phi,
        resid,
        theta_t,
    )
    return r_factor, new_theta.T, predicted.reshape(share)


def solution(mesh):
    return jax.shard_map(
        on_device,
        mesh=mesh,
        in_specs=(P("rows", None, None), P("rows"), P("rows"), P("rows"), P("rows"), P(), P(), P()),
        out_specs=(P(), P(), P(("rows", "cols"))),
        check_vma=False,
    )
```

```python
import functools
import math

import jax
import jax.numpy as jnp
from jax import lax
from jax.experimental import pallas as pl
from jax.experimental.pallas import tpu as pltpu
from jax.sharding import PartitionSpec as P

Y_ORDERS = [0, 1, 0, 2, 1, 0, 0, 0]
X_ORDERS = [0, 0, 1, 0, 1, 2, 0, 2]
SIGMAS = [1.5, 1.5, 1.5, 1.5, 1.5, 1.5, 3.0, 3.0]

F32 = jnp.float32
BF16 = jnp.bfloat16
NN = (((1,), (0,)), ((), ()))
NT = (((1,), (1,)), ((), ()))
VMEM = pl.BlockSpec(memory_space=pltpu.VMEM)
HBM = pl.BlockSpec(memory_space=pltpu.HBM)
SMEM = pl.BlockSpec(memory_space=pltpu.SMEM)
PACK = 168
CHUNK = 512
PACE = 1
AHEAD = 2
BLK = 64


def iota(shape, dim):
    return lax.broadcasted_iota(jnp.int32, shape, dim)


def kernel_scale(order, width):
    total = 0.0
    for t in range(-12, 13):
        e = math.exp(-t * t / (2.0 * width * width))
        if order == 1:
            e = -t / width**2 * e
        elif order == 2:
            e = (t * t / width**4 - 1.0 / width**2) * e
        total += e * e
    return 1.0 / math.sqrt(total)


def kernel_values(lag, order, width):
    e = jnp.exp(lag * lag * (-1.0 / (2.0 * width * width)))
    if order == 1:
        e = lag * (-1.0 / width**2) * e
    elif order == 2:
        e = (lag * lag * (1.0 / width**4) - 1.0 / width**2) * e
    return e * kernel_scale(order, width)


def split(a):
    hi = a.astype(BF16)
    return hi, (a - hi.astype(F32)).astype(BF16)


def dot(a, b, dims=NN):
    return lax.dot_general(a, b, dims, preferred_element_type=F32)


def dot3(a, b, dims=NN):
    ah, al = a if isinstance(a, tuple) else split(a)
    bh, bl = b if isinstance(b, tuple) else split(b)
    return dot(ah, bh, dims) + (dot(ah, bl, dims) + dot(al, bh, dims))


def dot_full(a, b, dims=NN):
    return lax.dot_general(
        a, b, dims, precision=lax.Precision.HIGHEST, preferred_element_type=F32
    )


mm = dot_full


def places(ncols):
    column = lax.axis_index("cols")
    if ncols == 2:
        return column, lax.axis_index("rows") & 1, column
    return (column >> 1) & 1, column & 1, column


def front(
    ncols,
    count_ref,
    img_hbm,
    pix_hbm,
    mask_hbm,
    target_hbm,
    theta_hbm,
    amp_hbm,
    keep_ref,
    send_ref,
    slope_ref,
    phi_ref,
    resid_ref,
    theta_out_ref,
    img_ref,
    pix_ref,
    mask_ref,
    target_ref,
    theta_ref,
    amp_ref,
    pick_ref,
    feat_ref,
    jac_ref,
    all_phi_ref,
    all_sr_ref,
    all_slope_ref,
    all_resid_ref,
    sem,
):
    pairs = [
        (img_hbm, img_ref),
        (pix_hbm, pix_ref),
        (theta_hbm, theta_ref),
        (amp_hbm, amp_ref),
        (mask_hbm, mask_ref),
        (target_hbm, target_ref),
    ]
    copies = [pltpu.make_async_copy(a, b, sem.at[i]) for i, (a, b) in enumerate(pairs)]
    for copy in copies:
        copy.start()
    half, quarter, column = places(ncols)
    count = count_ref[0]
    slots = pix_ref.shape[1]
    rows, breadth = img_ref.shape
    height = 32
    basis, chans = theta_ref.shape
    params = basis * chans

    kinds = sorted(set(zip(Y_ORDERS, SIGMAS)))
    tables = []
    for order, width in kinds:
        lag = ((iota((height, breadth), 1) & (height - 1)) - iota((height, breadth), 0)).astype(F32)
        table = kernel_values(lag, order, width)
        wide = jnp.concatenate([table] * (rows // height), 0)
        wide = jnp.concatenate([wide] * (rows // breadth), 1)
        same = (iota((rows, rows), 0) // height) == (iota((rows, rows), 1) // height)
        tables.append(split(jnp.where(same, wide, 0.0)))
    lag = (iota((breadth, breadth), 0) - iota((breadth, breadth), 1)).astype(F32)
    rights = [split(kernel_values(lag, X_ORDERS[k], SIGMAS[k])) for k in range(basis)]
    copies[1].wait()
    chunk = min(CHUNK, slots)
    for start in range(0, slots, chunk):
        row = pix_ref[:, start : start + chunk] // breadth
        pick = jnp.where(iota((rows, chunk), 0) == row, 1.0, 0.0).astype(BF16)
        pick_ref[:rows, start : start + chunk] = pick
        pick_ref[rows:, start : start + chunk] = pick
    copies[0].wait()
    image_t = split(img_ref[...].T)
    lefts = {kind: split(dot3(image_t, table)) for kind, table in zip(kinds, tables)}
    for k in range(basis):
        hi, lo = split(dot3(rights[k], lefts[Y_ORDERS[k], SIGMAS[k]]))
        feat_ref[k * breadth : (k + 1) * breadth, :rows] = hi
        feat_ref[k * breadth : (k + 1) * breadth, rows:] = lo

    for copy in copies[2:]:
        copy.wait()
    theta_out_ref[...] = theta_ref[...]
    theta = theta_ref[...].T
    diag = iota((chans, chans), 0) == iota((chans, chans), 1)
    amp = jnp.sum(jnp.where(diag, amp_ref[...], 0.0), axis=1, keepdims=True)

    live_total = jnp.zeros((1, 1), F32)
    for start in range(0, slots, chunk):
        at = slice(start, start + chunk)
        pick_col = iota((breadth, chunk), 0) == pix_ref[:, at] & (breadth - 1)
        phis = []
        for k in range(basis):
            found = dot(feat_ref[k * breadth : (k + 1) * breadth], pick_ref[:, at])
            phis.append(jnp.sum(jnp.where(pick_col, found, 0.0), axis=0, keepdims=True))
        phi = jnp.concatenate(phis, 0)
        all_phi_ref[:, at] = phi
        slot = iota((1, chunk), 1) + start
        live = jnp.where((slot < count) & (mask_ref[:, at] == 1), 1.0, 0.0)
        live_total = live_total + jnp.sum(live, axis=1, keepdims=True)
        z = theta[:, 0:1] * phis[0]
        for k in range(1, basis):
            z = z + theta[:, k : k + 1] * phis[k]
        act = jnp.tanh(z)
        model = jnp.sum(amp * act, axis=0, keepdims=True)
        resid = live * (model - target_ref[:, at])
        slope = (live * amp) * (1.0 - act * act)
        all_resid_ref[:, at] = resid
        all_slope_ref[:, at] = slope
        all_sr_ref[:, at] = slope * resid
        for k in range(basis):
            hi, lo = split(slope * phis[k])
            place = ((k + (basis // 2) * half) % basis) * chans
            jac_ref[pl.ds(pl.multiple_of(place, chans), chans), at] = hi
            jac_ref[pl.ds(pl.multiple_of(params + place, chans), chans), at] = lo

    own = slots // ncols
    mine = pl.ds(pl.multiple_of(column * own, own), own)
    slope_ref[...] = all_slope_ref[:, mine]
    phi_ref[...] = all_phi_ref[:, mine]
    resid_ref[...] = all_resid_ref[:, mine]

    grad = dot3(all_phi_ref[...], all_sr_ref[...], NT)

    four = basis // 2 * chans
    both = dot(jac_ref[:four], jac_ref[...], NT)
    low = dot(jac_ref[params : params + four], jac_ref[:params], NT)
    gram = both[:, :params] + (both[:, params:] + low)
    r = iota((chans, 128), 0)
    c = iota((chans, 128), 1) & (chans - 1)
    packs = []
    for part in range(2):
        tiles = [
            [
                gram[
                    (2 * part + e) * chans : (2 * part + e + 1) * chans,
                    (part + i) * 128 : (part + i + 1) * 128,
                ]
                for i in range(3)
            ]
            for e in range(2)
        ]
        spare = jnp.where(iota((chans, 128), 1) < chans, tiles[0][2], tiles[1][0])
        folds = []
        lost = []
        for one, two in (
            (tiles[0][0], tiles[0][1]),
            (tiles[1][1], tiles[1][2]),
            (spare, pltpu.roll(spare, chans, 1)),
        ):
            folds.append(jnp.where(r >= c, one, two))
            lost.append(jnp.sum(jnp.where(r == c, two, 0.0), axis=0, keepdims=True))
        last = folds.pop()
        folds.append(jnp.concatenate([last[: chans // 2, :chans], last[chans // 2 :, :chans]], 1))
        lost = [line[:, e * chans : (e + 1) * chans] for line in lost for e in range(2)][:5]
        lost += [jnp.broadcast_to(live_total, (1, chans)), jnp.zeros((2, chans), F32)]
        folds.append(jnp.concatenate([grad, jnp.concatenate(lost, 0)], 1))
        packs.append(folds)
    at = 0
    for one, two in zip(*packs):
        piece = pl.ds(at, one.shape[0])
        keep_ref[piece, :] = jnp.where(quarter == 0, one, two)
        send_ref[piece, :] = jnp.where(quarter == 0, two, one)
        at += one.shape[0]


def take(beside):
    while beside:
        try:
            next(beside[0])
            return True
        except StopIteration:
            beside.pop(0)
    return False


def factor_block(tiles, base, beside):
    count = len(tiles)
    tiles = list(tiles)
    sub = iota((8, 128), 0)
    inverses = []

    def spread(x):
        return jnp.broadcast_to(x, (8, 128))

    def column(t, at):
        return spread(tiles[t][:, at : at + 1])

    ahead = {}
    for g in range(count):
        near = range(g, min(g + 1 + AHEAD, count))
        far = range(near[-1] + 1, count)
        cols = {
            t: ahead[t] if t in ahead else [column(t, base + 8 * g + m) for m in range(8)]
            for t in range(g, count)
        }
        ahead = {t: [column(t, base + 8 * g + 8 + m) for m in range(8)] for t in near[1:]}
        kept = jnp.zeros((8, 128), F32)
        solved = tiles[g]
        for m in range(8):
            inverse = 1.0 / spread(cols[g][m][m : m + 1])
            kept = jnp.where(sub == m, inverse, kept)
            own = cols[g][m]
            for n in range(m + 1, 8):
                scaled = spread(cols[g][n][m : m + 1]) * inverse
                for t in near:
                    cols[t][n] = cols[t][n] - cols[t][m] * scaled
                if far:
                    cols[g][n] = jnp.where(sub == m, scaled, cols[g][n])
            mult = {t: cols[t][m] * inverse for t in near}
            mult[g] = jnp.where(sub > m, mult[g], 0.0)
            for n in range(8 if ahead else 0):
                pivot = spread(cols[g + 1][m][n : n + 1])
                for t in ahead:
                    ahead[t][n] = ahead[t][n] - mult[t] * pivot
            pivot = spread(tiles[g][m : m + 1])
            for t in near:
                tiles[t] = tiles[t] - mult[t] * pivot
            if far:
                pivot = spread(solved[m : m + 1]) * inverse
                solved = jnp.where(sub == m, pivot, solved - own * pivot)
        for m in range(8 if far else 0):
            pivot = spread(solved[m : m + 1])
            for t in far:
                tiles[t] = tiles[t] - cols[t][m] * pivot
        inverses.append(kept)
        if g % PACE == 0:
            beside()
    return tiles, inverses


def back(
    ncols,
    damping_ref,
    q0_ref,
    q1_ref,
    q2_ref,
    q3_ref,
    slope_ref,
    phi_ref,
    resid_ref,
    theta_ref,
    r_ref,
    new_theta_ref,
    pred_ref,
    pack_ref,
    plain_ref,
    mixed_ref,
    n_ref,
    t_ref,
    x_ref,
):
    half, quarter, _ = places(ncols)
    basis, chans = theta_ref.shape
    params = chans * basis
    pack_ref[2 * half + quarter] = q0_ref[...]
    pack_ref[2 * (1 - half) + quarter] = q1_ref[...]
    pack_ref[2 * half + (1 - quarter)] = q2_ref[...]
    pack_ref[2 * (1 - half) + (1 - quarter)] = q3_ref[...]

    total = pack_ref[0, PACK - 3 : PACK - 2, chans : chans + 1]
    scale = 1.0 / total
    r = iota((chans, chans), 0)
    c = iota((chans, chans), 1)

    def put(k, l, block):
        plain_ref[k * chans : (k + 1) * chans, l * chans : (l + 1) * chans] = block

    for q in range(4):
        lost = pack_ref[q, PACK - 8 :, chans:]
        for i in range(2):
            fold = pack_ref[q, i * chans : (i + 1) * chans, :]
            turned = fold.T
            k = 2 * q + i
            for e in range(2):
                lane = slice(e * chans, (e + 1) * chans)
                f, ft = fold[:, lane], turned[lane]
                second = jnp.where(r == c, lost[2 * i + e : 2 * i + e + 1], jnp.where(r < c, f, ft))
                for d, block in ((i + e, jnp.where(r >= c, f, ft)), (i + e + 2, second)):
                    l = (k + d) % basis
                    put(k, l, block)
                    if d not in (0, basis // 2):
                        put(l, k, block)
        last = pack_ref[q, 2 * chans : 2 * chans + chans // 2, :]
        f = jnp.concatenate([last[:, :chans], last[:, chans:]], 0)
        ft = f.T
        put(2 * q, (2 * q + basis // 2) % basis, jnp.where(r >= c, f, ft))
        second = jnp.where(r == c, lost[4:5], jnp.where(r < c, f, ft))
        put(2 * q + 1, 2 * q + 1, second)
    tiles = params // 128
    per = 128 // chans
    for k in range(basis):
        for b in range(tiles):
            mixed_ref[b, pl.ds(k, chans, stride=basis), :] = plain_ref[
                k * chans : (k + 1) * chans, b * 128 : (b + 1) * 128
            ]
    damping = damping_ref[0, 0]
    spot = iota((128, 128), 0) == iota((128, 128), 1)

    def fill(a):
        rows = (a + 1) * 128 // basis
        for b in range(tiles):
            t = mixed_ref[b, a * 128 : (a + 1) * 128, :].T * scale
            for e in range(per):
                n_ref[a, pl.ds(b * per + e, rows, stride=basis), :] = t[
                    e * chans : e * chans + rows
                ]
        at = slice(a * 128, (a + 1) * 128)
        n_ref[a, at, :] = n_ref[a, at, :] + jnp.where(spot, damping, 0.0)

    def fill_grad():
        grad = (pack_ref[0, PACK - 8 :, :] * scale).T[:chans]
        for k in range(basis):
            n_ref[tiles, pl.ds(k, chans, stride=basis), :] = jnp.broadcast_to(
                grad[:, k : k + 1], (chans, 128)
            )

    def fill_all():
        for a in range(1, tiles):
            fill(a)
            yield
        fill_grad()

    fill(0)
    beside = [fill_all()]

    lane = iota((BLK, 128), 1)
    sub = iota((BLK, 128), 0)
    zeros = jnp.zeros((BLK, 128), F32)

    def load(at, first):
        return jnp.concatenate([n_ref[t, at, :] for t in range(first, tiles + 1)], 1)

    def factor(block, base):
        eye = jnp.where(lane - (BLK - base) == sub, 1.0, 0.0)
        whole = jnp.where((lane >= base) & (lane < base + BLK), block, eye)
        parts = [whole[8 * t : 8 * t + 8] for t in range(BLK // 8)]
        parts, inverses = factor_block(parts, base, lambda: take(beside) or take(spare))
        return jnp.concatenate([p * (i * lax.rsqrt(i)) for p, i in zip(parts, inverses)], 0)

    def below(x):
        return jnp.concatenate([jnp.zeros(x.shape, F32), x], 0)

    def join(at, begin):
        return jnp.concatenate([n_ref[t, at, :] for t in range(begin, tiles + 1)], 1)

    def update(i, turned, part):
        at = slice(i * 128, (i + 1) * 128)
        change = mm(turned, part)
        begin = tiles + 1 - part.shape[1] // 128
        for t in range(begin, tiles + 1):
            n_ref[t, at, :] = n_ref[t, at, :] - change[:, (t - begin) * 128 :][:, :128]

    def early(j, top, low, inv0, cross, held):
        if j + 1 < tiles:
            held["near0"] = mm(inv0, below(n_ref[j + 1, top, :]))
            yield
            held["near_mid"] = n_ref[j + 1, low, :] - mm(cross, held["near0"])
            at = slice((j + 1) * 128, (j + 2) * 128)
            turned = held["near0"].T
            yield
            n_ref[j + 1, at, :] = n_ref[j + 1, at, :] - mm(turned, held["near0"])
            yield
        begin = min(j + 2, tiles)
        held["rest0"] = mm(inv0, below(join(top, begin)))
        yield
        held["middle"] = join(low, begin) - mm(cross, held["rest0"])
        yield

    def late(j, inv1, near, held):
        here = slice(j * 128, (j + 1) * 128)
        rest1 = mm(inv1, held["middle"])
        rest = jnp.concatenate([held["rest0"], rest1], 0)
        held["rest"] = rest
        if near is not None:
            held["rest"] = jnp.concatenate([near, rest], 1)
            turned = near.T
            yield
            update(j + 1, turned, rest)
            yield
            if j + 2 < tiles:
                r_ref[here, (j + 2) * 128 :] = rest[:, :-128]
            for i in range(j + 2, tiles):
                part = rest[:, (i - j - 2) * 128 :]
                update(i, part[:, :128].T, part)
                yield

    def solve(j, first, w0, w1, held):
        rest = held["rest"]
        turn1 = dot3(w1.T[:BLK], rest[BLK:])
        up0 = w0.T[BLK:]
        link = jnp.where(lane >= BLK, dot3(up0, first), 0.0)
        yield
        turn0 = dot3(up0, rest[:BLK]) - dot3(link, below(turn1))
        turn = jnp.concatenate([turn0, turn1], 0)
        for t in range(j + 1, tiles + 1):
            t_ref[j, t] = turn[:, (t - j - 1) * 128 : (t - j) * 128]

    spare = []
    for j in range(tiles):
        top = slice(j * 128, j * 128 + BLK)
        low = slice(j * 128 + BLK, (j + 1) * 128)
        here = slice(j * 128, (j + 1) * 128)
        w0 = factor(n_ref[j, top, :], 0)
        inv0 = jnp.where(lane >= BLK, w0, 0.0)
        first = mm(inv0, below(n_ref[j, top, :]))
        cross = first[:, BLK:].T
        held = {}
        beside.append(early(j, top, low, inv0, cross, held))
        w1 = factor(n_ref[j, low, :] - mm(cross, first), BLK)
        while take(beside):
            pass
        inv1 = w1[:, :BLK]
        near = None
        if j + 1 < tiles:
            near1 = mm(inv1, held["near_mid"])
            at = slice((j + 1) * 128, (j + 2) * 128)
            n_ref[j + 1, at, :] = n_ref[j + 1, at, :] - mm(near1.T, near1)
            near = jnp.concatenate([held["near0"], near1], 0)
            r_ref[here, at] = near
        if j:
            r_ref[here, : j * 128] = jnp.zeros((128, j * 128), F32)
        r_ref[top, here] = jnp.where(lane >= BLK, first, jnp.where(lane >= sub, w0, 0.0))
        r_ref[low, here] = jnp.where(lane - BLK >= sub, w1, 0.0)
        beside.append(late(j, inv1, near, held))
        spare.append(solve(j, first, w0, w1, held))
    while take(beside) or take(spare):
        pass

    for j in reversed(range(tiles)):
        x = t_ref[j, tiles]
        if j + 1 < tiles:
            x = x - dot3(
                jnp.concatenate([t_ref[j, t] for t in range(j + 1, tiles)], 1),
                x_ref[(j + 1) * 128 :, :],
            )
        x_ref[j * 128 : (j + 1) * 128, :] = x

    lane = iota((chans, 128), 1)
    weight = jnp.zeros(slope_ref.shape, F32)
    move = jnp.zeros((chans, 128), F32)
    width = slope_ref.shape[1]
    for k in range(basis):
        step = -x_ref[pl.ds(k, chans, stride=basis), :]
        move = jnp.where(lane == k, step, move)
        wide = jnp.concatenate([step] * (width // 128), 1)
        weight = weight + wide * phi_ref[k : k + 1, :]
    new_theta_ref[...] = theta_ref[...] + move.T[:basis]
    pred_ref[...] = resid_ref[...] + jnp.sum(slope_ref[...] * weight, axis=0, keepdims=True)


def on_device(images, gauge_pixel, row_mask, gauge_counts, targets, theta, amplitude, damping):
    nrows = lax.axis_size("rows")
    ncols = lax.axis_size("cols")
    slots = gauge_pixel.shape[0]
    share = slots // ncols
    chans, basis = theta.shape
    params = chans * basis
    breadth = images.shape[2]
    pixel_rows = images.shape[0] * images.shape[1]
    theta_t = theta.T
    shape = jax.ShapeDtypeStruct
    keep, send, slope, phi, resid, theta_here = pl.pallas_call(
        functools.partial(front, ncols),
        out_shape=[
            pltpu.VMEM((PACK, 128), F32),
            pltpu.VMEM((PACK, 128), F32),
            pltpu.VMEM((chans, share), F32),
            pltpu.VMEM((basis, share), F32),
            pltpu.VMEM((1, share), F32),
            pltpu.VMEM((basis, chans), F32),
        ],
        in_specs=[SMEM] + [HBM] * 6,
        out_specs=[VMEM] * 6,
        scratch_shapes=[
            pltpu.VMEM((pixel_rows, breadth), F32),
            pltpu.VMEM((1, slots), jnp.int32),
            pltpu.VMEM((1, slots), jnp.int32),
            pltpu.VMEM((1, slots), F32),
            pltpu.VMEM((basis, chans), F32),
            pltpu.VMEM((1, chans), F32),
            pltpu.VMEM((2 * pixel_rows, slots), BF16),
            pltpu.VMEM((basis * breadth, 2 * pixel_rows), BF16),
            pltpu.VMEM((2 * params, slots), BF16),
            pltpu.VMEM((basis, slots), F32),
            pltpu.VMEM((chans, slots), F32),
            pltpu.VMEM((chans, slots), F32),
            pltpu.VMEM((1, slots), F32),
            pltpu.SemaphoreType.DMA((6,)),
        ],
        compiler_params=pltpu.CompilerParams(vmem_limit_bytes=60 * 2**20),
        name="front",
    )(
        gauge_counts,
        images.reshape(pixel_rows, breadth),
        gauge_pixel.reshape(1, slots),
        row_mask.reshape(1, slots),
        targets.reshape(1, slots),
        theta_t,
        amplitude.reshape(1, chans),
    )

    def swap(x, row_bit, col_bit):
        pairs = [
            (r * ncols + c, (r ^ row_bit) * ncols + (c ^ col_bit))
            for r in range(nrows)
            for c in range(ncols)
        ]
        return lax.ppermute(x, ("rows", "cols"), pairs)

    bits = [1 << i for i in range(nrows.bit_length() - 1)]
    if ncols == 2:
        core, across = (1, 0), 1
        keep = keep + swap(send, *core)
        bits = bits[1:]
    else:
        core, across = (0, 1), 2
    last = bits.pop(max(len(bits) - 2, 0))
    for bit in bits:
        keep = keep + swap(keep, bit, 0)
    same, other, both = swap(keep, last, 0), swap(keep, 0, across), swap(keep, last, across)
    keep, other_half = keep + same, other + both
    other_quarter = swap(keep, *core)
    other_both = swap(other_half, *core)

    r_factor, new_theta, predicted = pl.pallas_call(
        functools.partial(back, ncols),
        out_shape=[
            shape((params, params), F32),
            shape((basis, chans), F32),
            shape((1, share), F32),
        ],
        in_specs=[SMEM] + [VMEM] * 8,
        out_specs=[VMEM] * 3,
        scratch_shapes=[
            pltpu.VMEM((4, PACK, 128), F32),
            pltpu.VMEM((params, params), F32),
            pltpu.VMEM((params // 128, params, 128), F32),
            pltpu.VMEM((params // 128 + 1, params, 128), F32),
            pltpu.VMEM((params // 128, params // 128 + 1, 128, 128), F32),
            pltpu.VMEM((params, 128), F32),
        ],
        compiler_params=pltpu.CompilerParams(vmem_limit_bytes=40 * 2**20),
        name="back",
    )(
        damping.reshape(1, 1),
        keep,
        other_half,
        other_quarter,
        other_both,
        slope,
        phi,
        resid,
        theta_here,
    )
    return r_factor, new_theta.T, predicted.reshape(share)


def solution(mesh):
    return jax.shard_map(
        on_device,
        mesh=mesh,
        in_specs=(P("rows", None, None), P("rows"), P("rows"), P("rows"), P("rows"), P(), P(), P()),
        out_specs=(P(), P(), P(("rows", "cols"))),
        check_vma=False,
    )
```

```python
import functools
import math

import jax
import jax.numpy as jnp
from jax import lax
from jax.experimental import pallas as pl
from jax.experimental.pallas import tpu as pltpu
from jax.sharding import PartitionSpec as P

Y_ORDERS = [0, 1, 0, 2, 1, 0, 0, 0]
X_ORDERS = [0, 0, 1, 0, 1, 2, 0, 2]
SIGMAS = [1.5, 1.5, 1.5, 1.5, 1.5, 1.5, 3.0, 3.0]

F32 = jnp.float32
BF16 = jnp.bfloat16
NN = (((1,), (0,)), ((), ()))
NT = (((1,), (1,)), ((), ()))
VMEM = pl.BlockSpec(memory_space=pltpu.VMEM)
HBM = pl.BlockSpec(memory_space=pltpu.HBM)
SMEM = pl.BlockSpec(memory_space=pltpu.SMEM)
PACK = 168
CHUNK = 256
PACE = 1
AHEAD = 2
BLK = 64


def iota(shape, dim):
    return lax.broadcasted_iota(jnp.int32, shape, dim)


def kernel_scale(order, width):
    total = 0.0
    for t in range(-12, 13):
        e = math.exp(-t * t / (2.0 * width * width))
        if order == 1:
            e = -t / width**2 * e
        elif order == 2:
            e = (t * t / width**4 - 1.0 / width**2) * e
        total += e * e
    return 1.0 / math.sqrt(total)


def kernel_values(lag, order, width):
    e = jnp.exp(lag * lag * (-1.0 / (2.0 * width * width)))
    if order == 1:
        e = lag * (-1.0 / width**2) * e
    elif order == 2:
        e = (lag * lag * (1.0 / width**4) - 1.0 / width**2) * e
    return e * kernel_scale(order, width)


def split(a):
    hi = a.astype(BF16)
    return hi, (a - hi.astype(F32)).astype(BF16)


def dot(a, b, dims=NN):
    return lax.dot_general(a, b, dims, preferred_element_type=F32)


def dot3(a, b, dims=NN):
    ah, al = a if isinstance(a, tuple) else split(a)
    bh, bl = b if isinstance(b, tuple) else split(b)
    return dot(ah, bh, dims) + (dot(ah, bl, dims) + dot(al, bh, dims))


def dot_full(a, b, dims=NN):
    return lax.dot_general(
        a, b, dims, precision=lax.Precision.HIGHEST, preferred_element_type=F32
    )


mm = dot_full


def places(ncols):
    column = lax.axis_index("cols")
    if ncols == 2:
        return column, lax.axis_index("rows") & 1, column
    return (column >> 1) & 1, column & 1, column


def front(
    ncols,
    count_ref,
    img_hbm,
    pix_hbm,
    mask_hbm,
    target_hbm,
    theta_hbm,
    amp_hbm,
    keep_ref,
    send_ref,
    slope_ref,
    phi_ref,
    resid_ref,
    theta_out_ref,
    img_ref,
    pix_ref,
    mask_ref,
    target_ref,
    theta_ref,
    amp_ref,
    pick_ref,
    feat_ref,
    jac_ref,
    all_phi_ref,
    all_sr_ref,
    all_slope_ref,
    all_resid_ref,
    sem,
):
    pairs = [
        (img_hbm, img_ref),
        (pix_hbm, pix_ref),
        (theta_hbm, theta_ref),
        (amp_hbm, amp_ref),
        (mask_hbm, mask_ref),
        (target_hbm, target_ref),
    ]
    copies = [pltpu.make_async_copy(a, b, sem.at[i]) for i, (a, b) in enumerate(pairs)]
    for copy in copies:
        copy.start()
    half, quarter, column = places(ncols)
    count = count_ref[0]
    slots = pix_ref.shape[1]
    rows, breadth = img_ref.shape
    height = 32
    basis, chans = theta_ref.shape
    params = basis * chans

    kinds = sorted(set(zip(Y_ORDERS, SIGMAS)))
    tables = []
    for order, width in kinds:
        lag = ((iota((height, breadth), 1) & (height - 1)) - iota((height, breadth), 0)).astype(F32)
        table = kernel_values(lag, order, width)
        wide = jnp.concatenate([table] * (rows // height), 0)
        wide = jnp.concatenate([wide] * (rows // breadth), 1)
        same = (iota((rows, rows), 0) // height) == (iota((rows, rows), 1) // height)
        tables.append(split(jnp.where(same, wide, 0.0)))
    lag = (iota((breadth, breadth), 0) - iota((breadth, breadth), 1)).astype(F32)
    rights = [split(kernel_values(lag, X_ORDERS[k], SIGMAS[k])) for k in range(basis)]
    copies[1].wait()
    chunk = min(CHUNK, slots)
    for start in range(0, slots, chunk):
        row = pix_ref[:, start : start + chunk] // breadth
        pick = jnp.where(iota((rows, chunk), 0) == row, 1.0, 0.0).astype(BF16)
        pick_ref[:rows, start : start + chunk] = pick
        pick_ref[rows:, start : start + chunk] = pick
    copies[0].wait()
    image_t = split(img_ref[...].T)
    lefts = {kind: split(dot3(image_t, table)) for kind, table in zip(kinds, tables)}
    for k in range(basis):
        hi, lo = split(dot3(rights[k], lefts[Y_ORDERS[k], SIGMAS[k]]))
        feat_ref[k * breadth : (k + 1) * breadth, :rows] = hi
        feat_ref[k * breadth : (k + 1) * breadth, rows:] = lo

    for copy in copies[2:]:
        copy.wait()
    theta_out_ref[...] = theta_ref[...]
    theta = theta_ref[...].T
    diag = iota((chans, chans), 0) == iota((chans, chans), 1)
    amp = jnp.sum(jnp.where(diag, amp_ref[...], 0.0), axis=1, keepdims=True)

    live_total = jnp.zeros((1, 1), F32)
    for start in range(0, slots, chunk):
        at = slice(start, start + chunk)
        pick_col = iota((breadth, chunk), 0) == pix_ref[:, at] & (breadth - 1)
        phis = []
        for k in range(basis):
            found = dot(feat_ref[k * breadth : (k + 1) * breadth], pick_ref[:, at])
            phis.append(jnp.sum(jnp.where(pick_col, found, 0.0), axis=0, keepdims=True))
        phi = jnp.concatenate(phis, 0)
        all_phi_ref[:, at] = phi
        slot = iota((1, chunk), 1) + start
        live = jnp.where((slot < count) & (mask_ref[:, at] == 1), 1.0, 0.0)
        live_total = live_total + jnp.sum(live, axis=1, keepdims=True)
        z = theta[:, 0:1] * phis[0]
        for k in range(1, basis):
            z = z + theta[:, k : k + 1] * phis[k]
        act = jnp.tanh(z)
        model = jnp.sum(amp * act, axis=0, keepdims=True)
        resid = live * (model - target_ref[:, at])
        slope = (live * amp) * (1.0 - act * act)
        all_resid_ref[:, at] = resid
        all_slope_ref[:, at] = slope
        all_sr_ref[:, at] = slope * resid
        for k in range(basis):
            hi, lo = split(slope * phis[k])
            place = ((k + (basis // 2) * half) % basis) * chans
            jac_ref[pl.ds(pl.multiple_of(place, chans), chans), at] = hi
            jac_ref[pl.ds(pl.multiple_of(params + place, chans), chans), at] = lo

    own = slots // ncols
    mine = pl.ds(pl.multiple_of(column * own, own), own)
    slope_ref[...] = all_slope_ref[:, mine]
    phi_ref[...] = all_phi_ref[:, mine]
    resid_ref[...] = all_resid_ref[:, mine]

    grad = dot3(all_phi_ref[...], all_sr_ref[...], NT)

    four = basis // 2 * chans
    both = dot(jac_ref[:four], jac_ref[...], NT)
    low = dot(jac_ref[params : params + four], jac_ref[:params], NT)
    gram = both[:, :params] + (both[:, params:] + low)
    r = iota((chans, 128), 0)
    c = iota((chans, 128), 1) & (chans - 1)
    packs = []
    for part in range(2):
        tiles = [
            [
                gram[
                    (2 * part + e) * chans : (2 * part + e + 1) * chans,
                    (part + i) * 128 : (part + i + 1) * 128,
                ]
                for i in range(3)
            ]
            for e in range(2)
        ]
        spare = jnp.where(iota((chans, 128), 1) < chans, tiles[0][2], tiles[1][0])
        folds = []
        lost = []
        for one, two in (
            (tiles[0][0], tiles[0][1]),
            (tiles[1][1], tiles[1][2]),
            (spare, pltpu.roll(spare, chans, 1)),
        ):
            folds.append(jnp.where(r >= c, one, two))
            lost.append(jnp.sum(jnp.where(r == c, two, 0.0), axis=0, keepdims=True))
        last = folds.pop()
        folds.append(jnp.concatenate([last[: chans // 2, :chans], last[chans // 2 :, :chans]], 1))
        lost = [line[:, e * chans : (e + 1) * chans] for line in lost for e in range(2)][:5]
        lost += [jnp.broadcast_to(live_total, (1, chans)), jnp.zeros((2, chans), F32)]
        folds.append(jnp.concatenate([grad, jnp.concatenate(lost, 0)], 1))
        packs.append(folds)
    at = 0
    for one, two in zip(*packs):
        piece = pl.ds(at, one.shape[0])
        keep_ref[piece, :] = jnp.where(quarter == 0, one, two)
        send_ref[piece, :] = jnp.where(quarter == 0, two, one)
        at += one.shape[0]


def take(beside):
    while beside:
        try:
            next(beside[0])
            return True
        except StopIteration:
            beside.pop(0)
    return False


def factor_block(tiles, base, beside):
    count = len(tiles)
    tiles = list(tiles)
    sub = iota((8, 128), 0)
    inverses = []

    def spread(x):
        return jnp.broadcast_to(x, (8, 128))

    def column(t, at):
        return spread(tiles[t][:, at : at + 1])

    ahead = {}
    for g in range(count):
        near = range(g, min(g + 1 + AHEAD, count))
        far = range(near[-1] + 1, count)
        cols = {
            t: ahead[t] if t in ahead else [column(t, base + 8 * g + m) for m in range(8)]
            for t in range(g, count)
        }
        ahead = {t: [column(t, base + 8 * g + 8 + m) for m in range(8)] for t in near[1:]}
        kept = jnp.zeros((8, 128), F32)
        solved = tiles[g]
        for m in range(8):
            inverse = 1.0 / spread(cols[g][m][m : m + 1])
            kept = jnp.where(sub == m, inverse, kept)
            own = cols[g][m]
            for n in range(m + 1, 8):
                scaled = spread(cols[g][n][m : m + 1]) * inverse
                for t in near:
                    cols[t][n] = cols[t][n] - cols[t][m] * scaled
                if far:
                    cols[g][n] = jnp.where(sub == m, scaled, cols[g][n])
            mult = {t: cols[t][m] * inverse for t in near}
            mult[g] = jnp.where(sub > m, mult[g], 0.0)
            for n in range(8 if ahead else 0):
                pivot = spread(cols[g + 1][m][n : n + 1])
                for t in ahead:
                    ahead[t][n] = ahead[t][n] - mult[t] * pivot
            pivot = spread(tiles[g][m : m + 1])
            for t in near:
                tiles[t] = tiles[t] - mult[t] * pivot
            if far:
                pivot = spread(solved[m : m + 1]) * inverse
                solved = jnp.where(sub == m, pivot, solved - own * pivot)
        for m in range(8 if far else 0):
            pivot = spread(solved[m : m + 1])
            for t in far:
                tiles[t] = tiles[t] - cols[t][m] * pivot
        inverses.append(kept)
        if g % PACE == 0:
            beside()
    return tiles, inverses


def back(
    ncols,
    damping_ref,
    q0_ref,
    q1_ref,
    q2_ref,
    q3_ref,
    slope_ref,
    phi_ref,
    resid_ref,
    theta_ref,
    r_ref,
    new_theta_ref,
    pred_ref,
    pack_ref,
    plain_ref,
    mixed_ref,
    n_ref,
    t_ref,
    x_ref,
):
    half, quarter, _ = places(ncols)
    basis, chans = theta_ref.shape
    params = chans * basis
    pack_ref[2 * half + quarter] = q0_ref[...]
    pack_ref[2 * (1 - half) + quarter] = q1_ref[...]
    pack_ref[2 * half + (1 - quarter)] = q2_ref[...]
    pack_ref[2 * (1 - half) + (1 - quarter)] = q3_ref[...]

    total = pack_ref[0, PACK - 3 : PACK - 2, chans : chans + 1]
    scale = 1.0 / total
    r = iota((chans, chans), 0)
    c = iota((chans, chans), 1)

    def put(k, l, block):
        plain_ref[k * chans : (k + 1) * chans, l * chans : (l + 1) * chans] = block

    for q in range(4):
        lost = pack_ref[q, PACK - 8 :, chans:]
        for i in range(2):
            fold = pack_ref[q, i * chans : (i + 1) * chans, :]
            turned = fold.T
            k = 2 * q + i
            for e in range(2):
                lane = slice(e * chans, (e + 1) * chans)
                f, ft = fold[:, lane], turned[lane]
                second = jnp.where(r == c, lost[2 * i + e : 2 * i + e + 1], jnp.where(r < c, f, ft))
                for d, block in ((i + e, jnp.where(r >= c, f, ft)), (i + e + 2, second)):
                    l = (k + d) % basis
                    put(k, l, block)
                    if d not in (0, basis // 2):
                        put(l, k, block)
        last = pack_ref[q, 2 * chans : 2 * chans + chans // 2, :]
        f = jnp.concatenate([last[:, :chans], last[:, chans:]], 0)
        ft = f.T
        put(2 * q, (2 * q + basis // 2) % basis, jnp.where(r >= c, f, ft))
        second = jnp.where(r == c, lost[4:5], jnp.where(r < c, f, ft))
        put(2 * q + 1, 2 * q + 1, second)
    tiles = params // 128
    per = 128 // chans
    for k in range(basis):
        for b in range(tiles):
            mixed_ref[b, pl.ds(k, chans, stride=basis), :] = plain_ref[
                k * chans : (k + 1) * chans, b * 128 : (b + 1) * 128
            ]
    damping = damping_ref[0, 0]
    spot = iota((128, 128), 0) == iota((128, 128), 1)

    def fill(a):
        rows = (a + 1) * 128 // basis
        for b in range(tiles):
            t = mixed_ref[b, a * 128 : (a + 1) * 128, :].T * scale
            for e in range(per):
                n_ref[a, pl.ds(b * per + e, rows, stride=basis), :] = t[
                    e * chans : e * chans + rows
                ]
        at = slice(a * 128, (a + 1) * 128)
        n_ref[a, at, :] = n_ref[a, at, :] + jnp.where(spot, damping, 0.0)

    def fill_grad():
        grad = (pack_ref[0, PACK - 8 :, :] * scale).T[:chans]
        for k in range(basis):
            n_ref[tiles, pl.ds(k, chans, stride=basis), :] = jnp.broadcast_to(
                grad[:, k : k + 1], (chans, 128)
            )

    def fill_all():
        for a in range(1, tiles):
            fill(a)
            yield
        fill_grad()

    fill(0)
    beside = [fill_all()]

    lane = iota((BLK, 128), 1)
    sub = iota((BLK, 128), 0)
    zeros = jnp.zeros((BLK, 128), F32)

    def load(at, first):
        return jnp.concatenate([n_ref[t, at, :] for t in range(first, tiles + 1)], 1)

    def factor(block, base):
        eye = jnp.where(lane - (BLK - base) == sub, 1.0, 0.0)
        whole = jnp.where((lane >= base) & (lane < base + BLK), block, eye)
        parts = [whole[8 * t : 8 * t + 8] for t in range(BLK // 8)]
        parts, inverses = factor_block(parts, base, lambda: take(beside) or take(spare))
        return jnp.concatenate([p * (i * lax.rsqrt(i)) for p, i in zip(parts, inverses)], 0)

    def below(x):
        return jnp.concatenate([jnp.zeros(x.shape, F32), x], 0)

    def join(at, begin):
        return jnp.concatenate([n_ref[t, at, :] for t in range(begin, tiles + 1)], 1)

    def update(i, turned, part):
        at = slice(i * 128, (i + 1) * 128)
        change = mm(turned, part)
        begin = tiles + 1 - part.shape[1] // 128
        for t in range(begin, tiles + 1):
            n_ref[t, at, :] = n_ref[t, at, :] - change[:, (t - begin) * 128 :][:, :128]

    def early(j, top, low, inv0, cross, held):
        if j + 1 < tiles:
            held["near0"] = mm(inv0, below(n_ref[j + 1, top, :]))
            yield
            held["near_mid"] = n_ref[j + 1, low, :] - mm(cross, held["near0"])
            at = slice((j + 1) * 128, (j + 2) * 128)
            turned = held["near0"].T
            yield
            n_ref[j + 1, at, :] = n_ref[j + 1, at, :] - mm(turned, held["near0"])
            yield
        begin = min(j + 2, tiles)
        held["rest0"] = mm(inv0, below(join(top, begin)))
        yield
        held["middle"] = join(low, begin) - mm(cross, held["rest0"])
        yield

    def late(j, inv1, near, held):
        here = slice(j * 128, (j + 1) * 128)
        rest1 = mm(inv1, held["middle"])
        rest = jnp.concatenate([held["rest0"], rest1], 0)
        held["rest"] = rest
        if near is not None:
            held["rest"] = jnp.concatenate([near, rest], 1)
            turned = near.T
            yield
            update(j + 1, turned, rest)
            yield
            if j + 2 < tiles:
                r_ref[here, (j + 2) * 128 :] = rest[:, :-128]
            for i in range(j + 2, tiles):
                part = rest[:, (i - j - 2) * 128 :]
                update(i, part[:, :128].T, part)
                yield

    def solve(j, first, w0, w1, held):
        rest = held["rest"]
        turn1 = dot3(w1.T[:BLK], rest[BLK:])
        up0 = w0.T[BLK:]
        link = jnp.where(lane >= BLK, dot3(up0, first), 0.0)
        yield
        turn0 = dot3(up0, rest[:BLK]) - dot3(link, below(turn1))
        turn = jnp.concatenate([turn0, turn1], 0)
        for t in range(j + 1, tiles + 1):
            t_ref[j, t] = turn[:, (t - j - 1) * 128 : (t - j) * 128]

    spare = []
    for j in range(tiles):
        top = slice(j * 128, j * 128 + BLK)
        low = slice(j * 128 + BLK, (j + 1) * 128)
        here = slice(j * 128, (j + 1) * 128)
        w0 = factor(n_ref[j, top, :], 0)
        inv0 = jnp.where(lane >= BLK, w0, 0.0)
        first = mm(inv0, below(n_ref[j, top, :]))
        cross = first[:, BLK:].T
        held = {}
        beside.append(early(j, top, low, inv0, cross, held))
        w1 = factor(n_ref[j, low, :] - mm(cross, first), BLK)
        while take(beside):
            pass
        inv1 = w1[:, :BLK]
        near = None
        if j + 1 < tiles:
            near1 = mm(inv1, held["near_mid"])
            at = slice((j + 1) * 128, (j + 2) * 128)
            n_ref[j + 1, at, :] = n_ref[j + 1, at, :] - mm(near1.T, near1)
            near = jnp.concatenate([held["near0"], near1], 0)
            r_ref[here, at] = near
        if j:
            r_ref[here, : j * 128] = jnp.zeros((128, j * 128), F32)
        r_ref[top, here] = jnp.where(lane >= BLK, first, jnp.where(lane >= sub, w0, 0.0))
        r_ref[low, here] = jnp.where(lane - BLK >= sub, w1, 0.0)
        beside.append(late(j, inv1, near, held))
        spare.append(solve(j, first, w0, w1, held))
    while take(beside) or take(spare):
        pass

    for j in reversed(range(tiles)):
        x = t_ref[j, tiles]
        if j + 1 < tiles:
            x = x - dot3(
                jnp.concatenate([t_ref[j, t] for t in range(j + 1, tiles)], 1),
                x_ref[(j + 1) * 128 :, :],
            )
        x_ref[j * 128 : (j + 1) * 128, :] = x

    lane = iota((chans, 128), 1)
    weight = jnp.zeros(slope_ref.shape, F32)
    move = jnp.zeros((chans, 128), F32)
    width = slope_ref.shape[1]
    for k in range(basis):
        step = -x_ref[pl.ds(k, chans, stride=basis), :]
        move = jnp.where(lane == k, step, move)
        wide = jnp.concatenate([step] * (width // 128), 1)
        weight = weight + wide * phi_ref[k : k + 1, :]
    new_theta_ref[...] = theta_ref[...] + move.T[:basis]
    pred_ref[...] = resid_ref[...] + jnp.sum(slope_ref[...] * weight, axis=0, keepdims=True)


def on_device(images, gauge_pixel, row_mask, gauge_counts, targets, theta, amplitude, damping):
    nrows = lax.axis_size("rows")
    ncols = lax.axis_size("cols")
    slots = gauge_pixel.shape[0]
    share = slots // ncols
    chans, basis = theta.shape
    params = chans * basis
    breadth = images.shape[2]
    pixel_rows = images.shape[0] * images.shape[1]
    theta_t = theta.T
    shape = jax.ShapeDtypeStruct
    keep, send, slope, phi, resid, theta_here = pl.pallas_call(
        functools.partial(front, ncols),
        out_shape=[
            pltpu.VMEM((PACK, 128), F32),
            pltpu.VMEM((PACK, 128), F32),
            pltpu.VMEM((chans, share), F32),
            pltpu.VMEM((basis, share), F32),
            pltpu.VMEM((1, share), F32),
            pltpu.VMEM((basis, chans), F32),
        ],
        in_specs=[SMEM] + [HBM] * 6,
        out_specs=[VMEM] * 6,
        scratch_shapes=[
            pltpu.VMEM((pixel_rows, breadth), F32),
            pltpu.VMEM((1, slots), jnp.int32),
            pltpu.VMEM((1, slots), jnp.int32),
            pltpu.VMEM((1, slots), F32),
            pltpu.VMEM((basis, chans), F32),
            pltpu.VMEM((1, chans), F32),
            pltpu.VMEM((2 * pixel_rows, slots), BF16),
            pltpu.VMEM((basis * breadth, 2 * pixel_rows), BF16),
            pltpu.VMEM((2 * params, slots), BF16),
            pltpu.VMEM((basis, slots), F32),
            pltpu.VMEM((chans, slots), F32),
            pltpu.VMEM((chans, slots), F32),
            pltpu.VMEM((1, slots), F32),
            pltpu.SemaphoreType.DMA((6,)),
        ],
        compiler_params=pltpu.CompilerParams(vmem_limit_bytes=60 * 2**20),
        name="front",
    )(
        gauge_counts,
        images.reshape(pixel_rows, breadth),
        gauge_pixel.reshape(1, slots),
        row_mask.reshape(1, slots),
        targets.reshape(1, slots),
        theta_t,
        amplitude.reshape(1, chans),
    )

    def swap(x, row_bit, col_bit):
        pairs = [
            (r * ncols + c, (r ^ row_bit) * ncols + (c ^ col_bit))
            for r in range(nrows)
            for c in range(ncols)
        ]
        return lax.ppermute(x, ("rows", "cols"), pairs)

    bits = [1 << i for i in range(nrows.bit_length() - 1)]
    if ncols == 2:
        core, across = (1, 0), 1
        keep = keep + swap(send, *core)
        bits = bits[1:]
    else:
        core, across = (0, 1), 2
    last = bits.pop(max(len(bits) - 2, 0))
    for bit in bits:
        keep = keep + swap(keep, bit, 0)
    same, other, both = swap(keep, last, 0), swap(keep, 0, across), swap(keep, last, across)
    keep, other_half = keep + same, other + both
    other_quarter = swap(keep, *core)
    other_both = swap(other_half, *core)

    r_factor, new_theta, predicted = pl.pallas_call(
        functools.partial(back, ncols),
        out_shape=[
            shape((params, params), F32),
            shape((basis, chans), F32),
            shape((1, share), F32),
        ],
        in_specs=[SMEM] + [VMEM] * 8,
        out_specs=[VMEM] * 3,
        scratch_shapes=[
            pltpu.VMEM((4, PACK, 128), F32),
            pltpu.VMEM((params, params), F32),
            pltpu.VMEM((params // 128, params, 128), F32),
            pltpu.VMEM((params // 128 + 1, params, 128), F32),
            pltpu.VMEM((params // 128, params // 128 + 1, 128, 128), F32),
            pltpu.VMEM((params, 128), F32),
        ],
        compiler_params=pltpu.CompilerParams(vmem_limit_bytes=40 * 2**20),
        name="back",
    )(
        damping.reshape(1, 1),
        keep,
        other_half,
        other_quarter,
        other_both,
        slope,
        phi,
        resid,
        theta_here,
    )
    return r_factor, new_theta.T, predicted.reshape(share)


def solution(mesh):
    return jax.shard_map(
        on_device,
        mesh=mesh,
        in_specs=(P("rows", None, None), P("rows"), P("rows"), P("rows"), P("rows"), P(), P(), P()),
        out_specs=(P(), P(), P(("rows", "cols"))),
        check_vma=False,
    )
```
